256 devices in a mesh: dp: 16 (over z_hi, y), tensor: 16 (over x, z_lo, core).
Axes of the slice: x: 4, y: 4, z: 8 (z_hi: 4, z_lo: 2; z = z_hi * 2 + z_lo), core: 2. Of those that a mesh axis runs over, the one named last changes fastest.
Arguments:
- tokens: bfloat16 [12288, 8192], P('dp', 'tensor'), may hold values from -6 to 6
- r_up: bfloat16 [16, 512, 1024], P('tensor', 'dp'), may hold values from -0.25 to 0.25
- l_up: bfloat16 [16, 1024, 1024], P('tensor', 'dp'), may hold values from -0.1875 to 0.1875
- r_down: bfloat16 [16, 1024, 1024], P('tensor', 'dp'), may hold values from -0.1875 to 0.1875
- l_down: bfloat16 [16, 1024, 512], P('tensor', 'dp'), may hold values from -0.1875 to 0.1875
- mask_r_up: int32 [16, 4, 8], P('tensor'), may hold values 0 or 1
- mask_l_up: int32 [16, 8, 8], P('tensor'), may hold values 0 or 1
- mask_r_down: int32 [16, 8, 8], P('tensor'), may hold values 0 or 1
- mask_l_down: int32 [16, 8, 4], P('tensor'), may hold values 0 or 1
- cotangent: bfloat16 [12288, 8192], P('dp', 'tensor'), may hold values from -6 to 6
Outputs:
- mixed: bfloat16 [12288, 8192], P('dp', 'tensor')
- tokens_grad: bfloat16 [12288, 8192], P('dp', 'tensor')
- r_up_grad: float32 [16, 512, 1024], P('tensor', 'dp')
- l_up_grad: float32 [16, 1024, 1024], P('tensor', 'dp')
- r_down_grad: float32 [16, 1024, 1024], P('tensor', 'dp')
- l_down_grad: float32 [16, 1024, 512], P('tensor', 'dp')
The draws below stay inside these ranges and needn't reach their ends.
Inputs may be any that keep to these rules, and one draw needn't show every extreme that they name: `mask_r_up`: 1 keeps a 128 x 128 tile of a factor's block, 0 drops it. `mask_l_up`: 1 keeps a 128 x 128 tile of a factor's block, 0 drops it. `mask_r_down`: 1 keeps a 128 x 128 tile of a factor's block, 0 drops it. `mask_l_down`: 1 keeps a 128 x 128 tile of a factor's block, 0 drops it.
All inputs are finite; a program needn't handle non-finite values.
Results may differ from the reference program's by a relative error of at most 0.018.
Values may be sent and summed in bfloat16 or wider, within the bound.
A program may use at most 128 MiB of HBM per device.

```python
import math
import jax
import jax.numpy as jnp
from jax import lax

BW = 512
FB = 1024
TILE = 128
TOK_DEV = 768
NB = 16
D = 8192
TOKENS = 12288
N_DP = 16


def place_ends(array, own_key, low, largest):
    longest = array.shape.index(max(array.shape))
    spots = []
    for shift in (0, 1):
        where = [jax.random.randint(jax.random.fold_in(own_key, axis), (), 0, length) for axis, length in enumerate(array.shape)]
        where[longest] = (where[longest] + shift) % array.shape[longest]
        spots.append(tuple(where))
    return array.at[spots[0]].set(low).at[spots[1]].set(largest)


def steps_of(stream_key, dims, shards, low, largest):
    def one(axis_at, parts):
        heights = jax.random.uniform(jax.random.fold_in(jax.random.fold_in(stream_key, 6), axis_at), (parts,), jnp.float32, low / len(shards), largest / len(shards))
        return jnp.repeat(jnp.exp(heights), dims[axis_at] // parts).reshape((-1,) + (1,) * (len(dims) - axis_at - 1))

    loudness = one(*shards[0])
    for cut in shards[1:]:
        loudness = loudness * one(*cut)
    return loudness


def scatter_about(key, dims, scale, limit, shards=(), held_as=jnp.bfloat16):
    drawn = scale * jax.random.normal(key, dims, jnp.float32)
    if shards:
        drawn = drawn * steps_of(key, dims, shards, -0.22, 0.18)
    return jnp.clip(drawn, -limit, limit).astype(held_as)


def setup_inputs(seed: int = 0) -> dict:
    key_list = jax.random.split(jax.random.key(seed), 11)
    tokens = scatter_about(key_list[0], (TOKENS, D), 1.0, 6.0, ((0, 16), (1, 16)))
    r_up = scatter_about(key_list[1], (NB, BW, FB), BW ** -0.5, 0.25, ((0, 16), (1, 16)))
    l_up = scatter_about(key_list[2], (NB, FB, FB), FB ** -0.5, 0.1875, ((0, 16), (1, 16)))
    r_down = scatter_about(key_list[3], (NB, FB, FB), FB ** -0.5, 0.1875, ((0, 16), (1, 16)))
    l_down = scatter_about(key_list[4], (NB, FB, BW), FB ** -0.5, 0.1875, ((0, 16), (1, 16)))
    mask_r_up = place_ends((jax.random.randint(key_list[5], (NB, BW // TILE, FB // TILE), 0, 4) < 3).astype(jnp.int32), jax.random.fold_in(key_list[5], 1), 0, 1)
    mask_l_up = place_ends((jax.random.randint(key_list[6], (NB, FB // TILE, FB // TILE), 0, 4) < 3).astype(jnp.int32), jax.random.fold_in(key_list[6], 1), 0, 1)
    mask_r_down = place_ends((jax.random.randint(key_list[7], (NB, FB // TILE, FB // TILE), 0, 4) < 3).astype(jnp.int32), jax.random.fold_in(key_list[7], 1), 0, 1)
    mask_l_down = place_ends((jax.random.randint(key_list[8], (NB, FB // TILE, BW // TILE), 0, 4) < 3).astype(jnp.int32), jax.random.fold_in(key_list[8], 1), 0, 1)
    cotangent = scatter_about(key_list[9], (TOKENS, D), 1.0, 6.0, ((0, 16), (1, 16)))
    return dict(tokens=tokens, r_up=r_up, l_up=l_up, r_down=r_down, l_down=l_down, mask_r_up=mask_r_up, mask_l_up=mask_l_up, mask_r_down=mask_r_down, mask_l_down=mask_l_down, cotangent=cotangent)


def masked(weight, mask):
    blocks, rows, cols = weight.shape
    row_tiles, col_tiles = (mask.shape[1], mask.shape[2])
    tiles = weight.reshape(blocks, row_tiles, rows // row_tiles, col_tiles, cols // col_tiles)
    tiles = tiles * mask[:, :, None, :, None].astype(weight.dtype)
    return tiles.reshape(blocks, rows, cols)

def blockwise(left, weight):
    return jnp.einsum('tbk,bkn->tbn', left.astype(jnp.float32), weight.astype(jnp.float32))

def blockwise_back(left, weight):
    return jnp.einsum('tbn,bkn->tbk', left.astype(jnp.float32), weight.astype(jnp.float32))

def permute(hidden):
    count, blocks, width = hidden.shape
    return hidden.reshape(count, blocks, blocks, width // blocks).swapaxes(1, 2).reshape(count, blocks, width)

def gelu_tanh(value):
    return jax.nn.gelu(value, approximate=True)

def grad_sum(left, right, mask, scale):
    count, blocks, inner = left.shape
    outer = right.shape[2]
    left_groups = left.reshape(N_DP, TOK_DEV, blocks, inner)
    right_groups = right.reshape(N_DP, TOK_DEV, blocks, outer)

    def step(total, pair):
        term = jnp.einsum('tbk,tbn->bkn', pair[0].astype(jnp.float32), pair[1].astype(jnp.float32)) * scale
        term = masked(term, mask).astype(jnp.bfloat16)
        term = lax.optimization_barrier(term)
        return (total + term.astype(jnp.float32), None)
    start = jnp.zeros((blocks, inner, outer), jnp.float32)
    total, unused = lax.scan(step, start, (left_groups, right_groups))
    return total

def reference(tokens, r_up, l_up, r_down, l_down, mask_r_up, mask_l_up, mask_r_down, mask_l_down, cotangent):
    blocks = r_up.shape[0]
    x_in = tokens.reshape(TOKENS, blocks, BW)
    d_out = cotangent.reshape(TOKENS, blocks, BW)
    w_r_up = masked(r_up, mask_r_up)
    w_l_up = masked(l_up, mask_l_up)
    w_r_down = masked(r_down, mask_r_down)
    w_l_down = masked(l_down, mask_l_down)
    first = blockwise(x_in, w_r_up).astype(jnp.bfloat16)
    moved = permute(first)
    inner = blockwise(moved, w_l_up)
    active = gelu_tanh(inner).astype(jnp.bfloat16)
    lowered = blockwise(active, w_r_down).astype(jnp.bfloat16)
    lowered_moved = permute(lowered)
    mixed = blockwise(lowered_moved, w_l_down).astype(jnp.bfloat16)
    d_lowered_moved = blockwise_back(d_out, w_l_down).astype(jnp.bfloat16)
    d_lowered = permute(d_lowered_moved)
    d_active = blockwise_back(d_lowered, w_r_down)
    unused, pull = jax.vjp(gelu_tanh, inner)
    d_inner = pull(d_active)[0].astype(jnp.bfloat16)
    d_moved = blockwise_back(d_inner, w_l_up).astype(jnp.bfloat16)
    d_first = permute(d_moved)
    tokens_grad = blockwise_back(d_first, w_r_up).astype(jnp.bfloat16)
    scale = 1.0 / math.sqrt(TOKENS)
    r_up_grad = grad_sum(x_in, d_first, mask_r_up, scale)
    l_up_grad = grad_sum(moved, d_inner, mask_l_up, scale)
    r_down_grad = grad_sum(active, d_lowered, mask_r_down, scale)
    l_down_grad = grad_sum(lowered_moved, d_out, mask_l_down, scale)
    return (mixed.reshape(TOKENS, blocks * BW), tokens_grad.reshape(TOKENS, blocks * BW), r_up_grad, l_up_grad, r_down_grad, l_down_grad)
```

```python
import math

import jax
import jax.numpy as jnp
from jax import lax
from jax.experimental import pallas as pl
from jax.experimental.pallas import tpu as pltpu
from jax.sharding import PartitionSpec as P

MESH = pl.DeviceIdType.MESH
BF = jnp.bfloat16
F32 = jnp.float32
TOK = 768
HID = 1024
WID = 512
GELU_A = math.sqrt(2.0 / math.pi)
GELU_B = 0.044715
SCALE = 1.0 / math.sqrt(12288.0)
SHARD = ((32, 1024), (64, 1024), (64, 1024), (64, 512))


def dot(a, b, ca, cb):
    return lax.dot_general(a, b, (((ca,), (cb,)), ((), ())), preferred_element_type=F32)


def block_kernel(
    tok_hbm,
    s_r_up,
    s_l_up,
    s_r_down,
    s_l_down,
    m_r_up,
    m_l_up,
    m_r_down,
    m_l_down,
    cot_hbm,
    mixed,
    tokens_grad,
    g_r_up,
    g_l_up,
    g_r_down,
    g_l_down,
    tok,
    tok_t,
    cot,
    w_0,
    w_1,
    w_2,
    w_3,
    p_0,
    p_1,
    p_2,
    p_3,
    h_0,
    h_1,
    h_2,
    h_3,
    st_0,
    st_1,
    st_2,
    st_3,
    u_0,
    u_1,
    u_2,
    u_3,
    act,
    slope,
    d_in,
    ra_0,
    ra_1,
    ra_2,
    ra_3,
    rb_0,
    rb_1,
    rb_2,
    rb_3,
    q_0,
    q_1,
    q_2,
    q_3,
    sa_0,
    sa_1,
    sa_2,
    sa_3,
    sb_0,
    sb_1,
    sb_2,
    sb_3,
    load_sem,
    ag_send,
    ag_recv,
    a_send,
    a_recv,
    b_send,
    b_recv,
    rs_send,
    rs_recv,
):
    shards = (s_r_up, s_l_up, s_r_down, s_l_down)
    masks = (m_r_up, m_l_up, m_r_down, m_l_down)
    grads = (g_r_up, g_l_up, g_r_down, g_l_down)
    w = (w_0, w_1, w_2, w_3)
    p = (p_0, p_1, p_2, p_3)
    h = (h_0, h_1, h_2, h_3)
    st = (st_0, st_1, st_2, st_3)
    u = (u_0, u_1, u_2, u_3)
    ra = (ra_0, ra_1, ra_2, ra_3)
    rb = (rb_0, rb_1, rb_2, rb_3)
    q = (q_0, q_1, q_2, q_3)
    sa = (sa_0, sa_1, sa_2, sa_3)
    sb = (sb_0, sb_1, sb_2, sb_3)

    d = lax.axis_index("dp")
    t = lax.axis_index("tensor")
    zh, y = d // 4, d % 4
    x, j = t // 4, t % 4
    zl, c = j // 2, j % 2
    zp, zm = (zh + 1) % 4, (zh + 3) % 4
    yp, ym = (y + 1) % 4, (y + 3) % 4
    zo, yo = (zh + 2) % 4, (y + 2) % 4
    z_dev = ((zp * 4 + y, t), (zm * 4 + y, t))
    y_dev = ((zh * 4 + yp, t), (zh * 4 + ym, t))
    js = [j] + [((zl + i // 2) % 2) * 2 + (c + i % 2) % 2 for i in (1, 2, 3)]
    j_dev = [None] + [(d, x * 4 + js[i]) for i in (1, 2, 3)]
    xs = [(x + k) % 4 for k in range(4)]
    x_dev = [None] + [(d, xs[k] * 4 + j) for k in (1, 2, 3)]

    loads = [
        pltpu.make_async_copy(tok_hbm, tok, load_sem.at[0]),
        pltpu.make_async_copy(cot_hbm, cot, load_sem.at[1]),
    ]
    for copy in loads:
        copy.start()

    barrier = pltpu.get_barrier_semaphore()
    partners = list(z_dev) + list(y_dev) + j_dev[1:] + x_dev[1:]
    for device in partners:
        pl.semaphore_signal(barrier, inc=1, device_id=device, device_id_type=MESH)

    sent = []

    def remote(src, dst, send, recv, device):
        return pltpu.make_async_remote_copy(
            src_ref=src,
            dst_ref=dst,
            send_sem=send,
            recv_sem=recv,
            device_id=device,
            device_id_type=MESH,
        )

    def start(src, dst, send, recv, device):
        copy = remote(src, dst, send, recv, device)
        copy.start()
        sent.append(copy)

    def tile_row(n):
        return (d * SHARD[n][0]) // 128

    def mask_shard(n):
        rows, cols = SHARD[n]
        for tile in range(cols // 128):
            keep = masks[n][0, tile_row(n), tile].astype(F32)
            part = shards[n][0, :, tile * 128 : (tile + 1) * 128].astype(F32) * keep
            w[n][zh, pl.ds(pl.multiple_of(y * rows, rows), rows), tile * 128 : (tile + 1) * 128] = part.astype(BF)

    def at_y(ref, n, lead, which, lo=0, size=None):
        rows = SHARD[n][0]
        size = rows if size is None else size
        return ref.at[lead, pl.ds(pl.multiple_of(which * rows + lo, 16), size), :]

    def ag_places(n, stage):
        half = SHARD[n][0] // 2
        if stage == 0:
            mine = at_y(w[n], n, zh, y)
            return (mine, mine), (at_y(w[n], n, zm, y), at_y(w[n], n, zp, y))
        if stage == 1:
            return (
                (at_y(w[n], n, zm, y, 0, half), at_y(w[n], n, zp, y, half, half)),
                (at_y(w[n], n, zo, y, 0, half), at_y(w[n], n, zo, y, half, half)),
            )
        full, low, high = pl.ds(0, 4), pl.ds(0, 2), pl.ds(2, 2)
        if stage == 2:
            mine = at_y(w[n], n, full, y)
            return (mine, mine), (at_y(w[n], n, full, ym), at_y(w[n], n, full, yp))
        return (
            (at_y(w[n], n, low, ym), at_y(w[n], n, high, yp)),
            (at_y(w[n], n, low, yo), at_y(w[n], n, high, yo)),
        )

    def ag_start(n, stage):
        out, _ = ag_places(n, stage)
        devices = z_dev if stage < 2 else y_dev
        for way in (0, 1):
            start(out[way], out[way], ag_send.at[n, stage, way], ag_recv.at[n, stage, way], devices[way])

    def ag_wait(n, stage):
        _, got = ag_places(n, stage)
        devices = z_dev if stage < 2 else y_dev
        for way in (0, 1):
            remote(got[way], got[way], ag_send.at[n, stage, way], ag_recv.at[n, stage, way], devices[way]).wait_recv()

    def chunk(ref, lead, which):
        return ref.at[lead, pl.ds(pl.multiple_of(which * 64, 64), 64), :]

    def a_start(n, k):
        lead = xs[k]
        for i in (1, 2, 3):
            dst = chunk(u[n], x, j) if k == 0 else chunk(st[n], lead, j)
            start(chunk(h[n], lead, js[i]), dst, a_send.at[n, k, i - 1], a_recv.at[n, k, i - 1], j_dev[i])

    def a_wait(n, k):
        lead = xs[k]
        for i in (1, 2, 3):
            dst = chunk(u[n], x, js[i]) if k == 0 else chunk(st[n], lead, js[i])
            remote(dst, dst, a_send.at[n, k, i - 1], a_recv.at[n, k, i - 1], j_dev[i]).wait_recv()

    def own_chunks(n):
        for k in range(4):
            dst = u[n] if k == 0 else st[n]
            rows = pl.ds(pl.multiple_of(j * 64, 64), 64)
            dst[xs[k], rows, :] = h[n][xs[k], rows, :]

    def b_start(n, k):
        start(st[n].at[xs[k]], u[n].at[x], b_send.at[n, k - 1], b_recv.at[n, k - 1], x_dev[k])

    def b_wait(n, k):
        dst = u[n].at[xs[4 - k]]
        remote(dst, dst, b_send.at[n, k - 1], b_recv.at[n, k - 1], x_dev[k]).wait_recv()

    def rs_places(n, stage):
        half = SHARD[n][0] // 2
        if stage == 0:
            return (
                (at_y(p[n], n, pl.ds(0, 2), yo), at_y(p[n], n, pl.ds(2, 2), yo)),
                (ra[n].at[0, pl.ds(0, 2)], ra[n].at[1, pl.ds(0, 2)]),
            )
        if stage == 1:
            return (
                (at_y(p[n], n, pl.ds(0, 4), yp), at_y(p[n], n, pl.ds(0, 4), ym)),
                (rb[n].at[0], rb[n].at[1]),
            )
        if stage == 2:
            return (
                (q[n].at[zo, pl.ds(0, half)], q[n].at[zo, pl.ds(half, half)]),
                (sa[n].at[0], sa[n].at[1]),
            )
        return (q[n].at[zp], q[n].at[zm]), (sb[n].at[0], sb[n].at[1])

    def rs_start(n, stage):
        out, into = rs_places(n, stage)
        devices = y_dev if stage < 2 else z_dev
        for way in (0, 1):
            start(out[way], into[way], rs_send.at[n, stage, way], rs_recv.at[n, stage, way], devices[way])

    def rs_wait(n, stage):
        _, into = rs_places(n, stage)
        devices = y_dev if stage < 2 else z_dev
        for way in (0, 1):
            remote(into[way], into[way], rs_send.at[n, stage, way], rs_recv.at[n, stage, way], devices[way]).wait_recv()

    def rs_add(n, stage):
        rows, _ = SHARD[n]
        half = rows // 2

        def at(which):
            return pl.ds(pl.multiple_of(which * rows, rows), rows)

        if stage == 0:
            for way, (lead, which) in enumerate(((0, yp), (2, ym))):
                for i in (0, 1):
                    total = p[n][lead + i, at(which), :].astype(F32) + ra[n][way, i].astype(F32)
                    p[n][lead + i, at(which), :] = total.astype(BF)
        elif stage == 1:
            for i in range(4):
                total = p[n][i, at(y), :].astype(F32) + rb[n][0, i].astype(F32) + rb[n][1, i].astype(F32)
                q[n][i] = total.astype(BF)
        elif stage == 2:
            for way, (which, lo) in enumerate(((zp, 0), (zm, half))):
                total = q[n][which, lo : lo + half, :].astype(F32) + sa[n][way].astype(F32)
                q[n][which, lo : lo + half, :] = total.astype(BF)
        else:
            _, cols = SHARD[n]
            for tile in range(cols // 128):
                at_cols = slice(tile * 128, (tile + 1) * 128)
                keep = masks[n][0, tile_row(n), tile].astype(F32) * SCALE
                total = q[n][zh, :, at_cols].astype(F32) + sb[n][0, :, at_cols].astype(F32) + sb[n][1, :, at_cols].astype(F32)
                grads[n][:, at_cols] = total * keep

    def rs_step(n, stage):
        rs_wait(n, stage)
        rs_add(n, stage)
        if stage < 3:
            rs_start(n, stage + 1)

    def columns(n, k):
        part = w[n][:, :, pl.ds(pl.multiple_of(k * 256, 256), 256)]
        return part.reshape(part.shape[0] * part.shape[1], 256)

    def whole(ref):
        return ref[...].reshape(HID, ref.shape[-1])

    def each(count, step):
        lax.fori_loop(0, count, lambda k, carry: (step(k), carry)[1], 0)

    mask_shard(0)
    mask_shard(3)
    pl.semaphore_wait(barrier, len(partners))
    ag_start(0, 0)
    ag_start(3, 0)
    mask_shard(1)
    mask_shard(2)
    for copy in loads:
        copy.wait()
    tok_t[...] = tok[...].T
    for n in (0, 3):
        ag_wait(n, 0)
        ag_start(n, 1)
    ag_start(1, 0)
    ag_start(2, 0)
    for n in (0, 3):
        ag_wait(n, 1)
        ag_start(n, 2)
    for n in (1, 2):
        ag_wait(n, 0)
        ag_start(n, 1)
    for n in (0, 3):
        ag_wait(n, 2)
        ag_start(n, 3)
    for n in (1, 2):
        ag_wait(n, 1)
    ag_wait(0, 3)
    ag_start(1, 2)
    ag_start(2, 2)

    def first(k):
        h[0][k] = dot(columns(0, k), tok_t[...], 0, 0).astype(BF)

    each(4, first)
    own_chunks(0)
    a_start(0, 1)
    a_start(0, 2)
    ag_wait(3, 3)

    def back_first(k):
        h[1][k] = dot(w[3][k], cot[...], 1, 1).astype(BF)

    each(4, back_first)
    own_chunks(1)
    order = [(n, k) for n in (0, 1) for k in (1, 2, 3, 0)]

    def exchange(order, ahead, after):
        for at, (n, k) in enumerate(order):
            a_wait(n, k)
            if k:
                b_start(n, k)
            if at + ahead < len(order):
                a_start(*order[at + ahead])
            for step in after.get(at, ()):
                step()

    def more_factors():
        for n in (1, 2):
            ag_wait(n, 2)
            ag_start(n, 3)

    exchange(order, 2, {5: (more_factors,)})

    for k in (1, 2, 3):
        b_wait(0, k)
    ag_wait(1, 3)

    def inner(k):
        v = dot(columns(1, k), whole(u[0]), 0, 0)
        vv = v * v
        tanh = jnp.tanh(GELU_A * (v + GELU_B * (vv * v)))
        up = 0.5 * (1.0 + tanh)
        act[k] = (v * up).astype(BF)
        slope[k] = up + 0.5 * v * (1.0 - tanh * tanh) * (GELU_A * (1.0 + (3.0 * GELU_B) * vv))

    each(4, inner)
    ag_wait(2, 3)

    def lowered(k):
        h[2][k] = dot(columns(2, k), whole(act), 0, 0).astype(BF)

    each(4, lowered)
    own_chunks(2)
    a_start(2, 1)
    a_start(2, 2)

    for k in (1, 2, 3):
        b_wait(1, k)

    def d_inner(k):
        d_in[k] = (dot(w[2][k], whole(u[1]), 1, 0) * slope[k]).astype(BF)

    each(4, d_inner)

    def d_moved(k):
        h[3][k] = dot(w[1][k], whole(d_in), 1, 0).astype(BF)

    each(4, d_moved)
    own_chunks(3)

    def grad_r_down(k):
        p[2][k] = dot(act[k], whole(u[1]), 1, 1).astype(BF)

    def grad_l_up(k):
        p[1][k] = dot(u[0][k], whole(d_in), 1, 1).astype(BF)

    def send_r_down():
        each(4, grad_r_down)
        rs_start(2, 0)

    def send_l_up():
        each(4, grad_l_up)
        rs_start(1, 0)

    order = [(n, k) for n in (2, 3) for k in (1, 2, 3, 0)]
    exchange(
        order,
        2,
        {
            0: (send_r_down,),
            1: (send_l_up,),
            4: (lambda: rs_step(2, 0),),
            5: (lambda: rs_step(1, 0),),
        },
    )

    for k in (1, 2, 3):
        b_wait(2, k)

    def grad_l_down(k):
        p[3][k] = dot(u[2][k], cot[...], 1, 0).astype(BF)

    each(4, grad_l_down)
    rs_start(3, 0)

    def mix(k):
        cols = pl.ds(pl.multiple_of(k * 256, 256), 256)
        part = u[2][:, :, cols].reshape(HID, 256)
        mixed[cols, :] = dot(part, whole(w[3]), 0, 0).astype(BF)

    each(3, mix)
    for k in (1, 2, 3):
        b_wait(3, k)

    def grad_r_up(k):
        rows = pl.ds(pl.multiple_of(k * 128, 128), 128)
        p[0][k] = dot(tok_t[rows, :], whole(u[3]), 1, 1).astype(BF)

    each(4, grad_r_up)
    rs_start(0, 0)

    def tok_grad(k):
        part = dot(w[0][k], whole(u[3]), 1, 0)
        tokens_grad[:, pl.ds(pl.multiple_of(k * 128, 128), 128)] = part.T.astype(BF)

    each(4, tok_grad)
    rs_step(2, 1)
    rs_step(3, 0)
    rs_step(1, 1)
    rs_step(0, 0)
    rs_step(2, 2)
    rs_step(1, 2)
    rs_step(3, 1)
    rs_step(0, 1)
    rs_step(2, 3)
    rs_step(1, 3)
    rs_step(3, 2)
    rs_step(0, 2)
    rs_step(3, 3)
    rs_step(0, 3)
    for copy in sent:
        copy.wait_send()


def per_device(*args):
    vmem = pl.BlockSpec(memory_space=pltpu.VMEM)
    smem = pl.BlockSpec(memory_space=pltpu.SMEM)
    anywhere = pl.BlockSpec(memory_space=pl.ANY)
    hidden = [pltpu.VMEM((4, 256, TOK), BF)]
    full = [pltpu.VMEM((4, 4 * rows, cols), BF) for rows, cols in SHARD]
    scratch = (
        [pltpu.VMEM((TOK, WID), BF), pltpu.VMEM((WID, TOK), BF), pltpu.VMEM((TOK, WID), BF)]
        + full * 2
        + hidden * 13
        + [pltpu.VMEM((4, 256, TOK), F32)]
        + hidden
        + [pltpu.VMEM((2, 2, rows, cols), BF) for rows, cols in SHARD]
        + [pltpu.VMEM((2, 4, rows, cols), BF) for rows, cols in SHARD]
        + [pltpu.VMEM((4, rows, cols), BF) for rows, cols in SHARD]
        + [pltpu.VMEM((2, rows // 2, cols), BF) for rows, cols in SHARD]
        + [pltpu.VMEM((2, rows, cols), BF) for rows, cols in SHARD]
        + [pltpu.SemaphoreType.DMA((2,))]
        + [pltpu.SemaphoreType.DMA((4, 4, 2))] * 2
        + [pltpu.SemaphoreType.DMA((4, 4, 3))] * 2
        + [pltpu.SemaphoreType.DMA((4, 3))] * 2
        + [pltpu.SemaphoreType.DMA((4, 4, 2))] * 2
    )
    outs = pl.pallas_call(
        block_kernel,
        name="block",
        out_shape=(
            jax.ShapeDtypeStruct((TOK, WID), BF),
            jax.ShapeDtypeStruct((TOK, WID), BF),
            *(jax.ShapeDtypeStruct(shape, F32) for shape in SHARD),
        ),
        in_specs=[anywhere] + [vmem] * 4 + [smem] * 4 + [anywhere],
        out_specs=(vmem,) * 6,
        scratch_shapes=scratch,
        compiler_params=pltpu.CompilerParams(
            collective_id=0, has_side_effects=True, vmem_limit_bytes=60 * 2**20
        ),
        cost_estimate=pl.CostEstimate(
            flops=15_000_000_000, bytes_accessed=8_000_000, transcendentals=800_000
        ),
    )(*args)
    return (outs[0], outs[1], *(g[None] for g in outs[2:]))


def solution(mesh):
    weight = P("tensor", "dp", None)
    mask = P("tensor", None, None)
    act = P("dp", "tensor")
    return jax.shard_map(
        per_device,
        mesh=mesh,
        in_specs=(act, weight, weight, weight, weight, mask, mask, mask, mask, act),
        out_specs=(act, act, weight, weight, weight, weight),
        check_vma=False,
    )
```

```python
import math

import jax
import jax.numpy as jnp
from jax import lax
from jax.experimental import pallas as pl
from jax.experimental.pallas import tpu as pltpu
from jax.sharding import PartitionSpec as P

MESH = pl.DeviceIdType.MESH
BF = jnp.bfloat16
F32 = jnp.float32
TOK = 768
HID = 1024
WID = 512
GELU_A = math.sqrt(2.0 / math.pi)
GELU_B = 0.044715
SCALE = 1.0 / math.sqrt(12288.0)
SHARD = ((32, 1024), (64, 1024), (64, 1024), (64, 512))


def dot(a, b, ca, cb):
    return lax.dot_general(a, b, (((ca,), (cb,)), ((), ())), preferred_element_type=F32)


def block_kernel(
    tok_hbm,
    s_r_up,
    s_l_up,
    s_r_down,
    s_l_down,
    m_r_up,
    m_l_up,
    m_r_down,
    m_l_down,
    cot_hbm,
    mixed,
    tokens_grad,
    g_r_up,
    g_l_up,
    g_r_down,
    g_l_down,
    tok,
    tok_t,
    cot,
    w_0,
    w_1,
    w_2,
    w_3,
    p_0,
    p_1,
    p_2,
    p_3,
    h_0,
    h_1,
    h_2,
    h_3,
    st_0,
    st_1,
    st_2,
    st_3,
    u_0,
    u_1,
    u_2,
    u_3,
    act,
    slope,
    d_in,
    ra_0,
    ra_1,
    ra_2,
    ra_3,
    rb_0,
    rb_1,
    rb_2,
    rb_3,
    q_0,
    q_1,
    q_2,
    q_3,
    sa_0,
    sa_1,
    sa_2,
    sa_3,
    sb_0,
    sb_1,
    sb_2,
    sb_3,
    load_sem,
    ag_send,
    ag_recv,
    a_send,
    a_recv,
    b_send,
    b_recv,
    rs_send,
    rs_recv,
):
    shards = (s_r_up, s_l_up, s_r_down, s_l_down)
    masks = (m_r_up, m_l_up, m_r_down, m_l_down)
    grads = (g_r_up, g_l_up, g_r_down, g_l_down)
    w = (w_0, w_1, w_2, w_3)
    p = (p_0, p_1, p_2, p_3)
    h = (h_0, h_1, h_2, h_3)
    st = (st_0, st_1, st_2, st_3)
    u = (u_0, u_1, u_2, u_3)
    ra = (ra_0, ra_1, ra_2, ra_3)
    rb = (rb_0, rb_1, rb_2, rb_3)
    q = (q_0, q_1, q_2, q_3)
    sa = (sa_0, sa_1, sa_2, sa_3)
    sb = (sb_0, sb_1, sb_2, sb_3)

    d = lax.axis_index("dp")
    t = lax.axis_index("tensor")
    zh, y = d // 4, d % 4
    x, j = t // 4, t % 4
    zl, c = j // 2, j % 2
    zp, zm = (zh + 1) % 4, (zh + 3) % 4
    yp, ym = (y + 1) % 4, (y + 3) % 4
    zo, yo = (zh + 2) % 4, (y + 2) % 4
    z_dev = ((zp * 4 + y, t), (zm * 4 + y, t))
    y_dev = ((zh * 4 + yp, t), (zh * 4 + ym, t))
    js = [j] + [((zl + i // 2) % 2) * 2 + (c + i % 2) % 2 for i in (1, 2, 3)]
    j_dev = [None] + [(d, x * 4 + js[i]) for i in (1, 2, 3)]
    xs = [(x + k) % 4 for k in range(4)]
    x_dev = [None] + [(d, xs[k] * 4 + j) for k in (1, 2, 3)]

    loads = [
        pltpu.make_async_copy(tok_hbm, tok, load_sem.at[0]),
        pltpu.make_async_copy(cot_hbm, cot, load_sem.at[1]),
    ]
    for copy in loads:
        copy.start()

    barrier = pltpu.get_barrier_semaphore()
    partners = list(z_dev) + list(y_dev) + j_dev[1:] + x_dev[1:]
    for device in partners:
        pl.semaphore_signal(barrier, inc=1, device_id=device, device_id_type=MESH)

    sent = []

    def remote(src, dst, send, recv, device):
        return pltpu.make_async_remote_copy(
            src_ref=src,
            dst_ref=dst,
            send_sem=send,
            recv_sem=recv,
            device_id=device,
            device_id_type=MESH,
        )

    def start(src, dst, send, recv, device):
        copy = remote(src, dst, send, recv, device)
        copy.start()
        sent.append(copy)

    def tile_row(n):
        return (d * SHARD[n][0]) // 128

    def mask_at(n, tile):
        if n == 3:
            return masks[n][0, tile, tile_row(n)]
        return masks[n][0, tile_row(n), tile]

    def mask_shard(n):
        rows, cols = SHARD[n]
        for tile in range(cols // 128):
            keep = mask_at(n, tile).astype(F32)
            part = shards[n][0, :, tile * 128 : (tile + 1) * 128].astype(F32) * keep
            w[n][zh, pl.ds(pl.multiple_of(y * rows, rows), rows), tile * 128 : (tile + 1) * 128] = part.astype(BF)

    def at_y(ref, n, lead, which, lo=0, size=None):
        rows = SHARD[n][0]
        size = rows if size is None else size
        return ref.at[lead, pl.ds(pl.multiple_of(which * rows + lo, 16), size), :]

    near = (zh, zm, zp, zo)

    def ag_moves(n, stage, r=0):
        half = SHARD[n][0] // 2

        def at(lead, which, *part):
            return at_y(w[n], n, lead, which, *part)

        if stage == "z1":
            mine = at(zh, y)
            return ((mine, at(zm, y), 0, z_dev[0]), (mine, at(zp, y), 1, z_dev[1]))
        if stage == "z2":
            return (
                (at(zm, y, 0, half), at(zo, y, 0, half), 2, z_dev[0]),
                (at(zp, y, half, half), at(zo, y, half, half), 3, z_dev[1]),
            )
        lead = near[r]
        if stage == "y1":
            mine = at(lead, y)
            return ((mine, at(lead, ym), 4 + 2 * r, y_dev[0]), (mine, at(lead, yp), 5 + 2 * r, y_dev[1]))
        way = r % 2
        return ((at(lead, (ym, yp)[way]), at(lead, yo), 12 + r, y_dev[way]),)

    def ag_start(n, stage, *places):
        for r in places or (0,):
            for src, _, sem, device in ag_moves(n, stage, r):
                start(src, src, ag_send.at[n, sem], ag_recv.at[n, sem], device)

    def ag_wait(n, stage, *places):
        for r in places or (0,):
            for _, dst, sem, device in ag_moves(n, stage, r):
                remote(dst, dst, ag_send.at[n, sem], ag_recv.at[n, sem], device).wait_recv()

    def ag_pass(n, *places):
        for r in places:
            ag_wait(n, "y1", r)
            ag_start(n, "y2", r)

    def chunk(ref, lead, which):
        return ref.at[lead, pl.ds(pl.multiple_of(which * 64, 64), 64), :]

    def a_start(n, k):
        lead = xs[k]
        for i in (1, 2, 3):
            dst = chunk(u[n], x, j) if k == 0 else chunk(st[n], lead, j)
            start(chunk(h[n], lead, js[i]), dst, a_send.at[n, k, i - 1], a_recv.at[n, k, i - 1], j_dev[i])

    def a_wait(n, k):
        lead = xs[k]
        for i in (1, 2, 3):
            dst = chunk(u[n], x, js[i]) if k == 0 else chunk(st[n], lead, js[i])
            remote(dst, dst, a_send.at[n, k, i - 1], a_recv.at[n, k, i - 1], j_dev[i]).wait_recv()

    def own_chunks(n):
        for k in range(4):
            dst = u[n] if k == 0 else st[n]
            rows = pl.ds(pl.multiple_of(j * 64, 64), 64)
            dst[xs[k], rows, :] = h[n][xs[k], rows, :]

    def b_start(n, k):
        start(st[n].at[xs[k]], u[n].at[x], b_send.at[n, k - 1], b_recv.at[n, k - 1], x_dev[k])

    def b_wait(n, k):
        dst = u[n].at[xs[4 - k]]
        remote(dst, dst, b_send.at[n, k - 1], b_recv.at[n, k - 1], x_dev[k]).wait_recv()

    def rs_places(n, stage):
        half = SHARD[n][0] // 2
        if stage == 0:
            return (
                (at_y(p[n], n, pl.ds(0, 2), yo), at_y(p[n], n, pl.ds(2, 2), yo)),
                (ra[n].at[0, pl.ds(0, 2)], ra[n].at[1, pl.ds(0, 2)]),
            )
        if stage == 1:
            return (
                (at_y(p[n], n, pl.ds(0, 4), yp), at_y(p[n], n, pl.ds(0, 4), ym)),
                (rb[n].at[0], rb[n].at[1]),
            )
        if stage == 2:
            return (
                (q[n].at[zo, pl.ds(0, half)], q[n].at[zo, pl.ds(half, half)]),
                (sa[n].at[0], sa[n].at[1]),
            )
        return (q[n].at[zp], q[n].at[zm]), (sb[n].at[0], sb[n].at[1])

    def rs_start(n, stage):
        out, into = rs_places(n, stage)
        devices = y_dev if stage < 2 else z_dev
        for way in (0, 1):
            start(out[way], into[way], rs_send.at[n, stage, way], rs_recv.at[n, stage, way], devices[way])

    def rs_wait(n, stage):
        _, into = rs_places(n, stage)
        devices = y_dev if stage < 2 else z_dev
        for way in (0, 1):
            remote(into[way], into[way], rs_send.at[n, stage, way], rs_recv.at[n, stage, way], devices[way]).wait_recv()

    def rs_add(n, stage):
        rows, _ = SHARD[n]
        half = rows // 2

        def at(which):
            return pl.ds(pl.multiple_of(which * rows, rows), rows)

        if stage == 0:
            for way, (lead, which) in enumerate(((0, yp), (2, ym))):
                for i in (0, 1):
                    total = p[n][lead + i, at(which), :].astype(F32) + ra[n][way, i].astype(F32)
                    p[n][lead + i, at(which), :] = total.astype(BF)
        elif stage == 1:
            for i in range(4):
                total = p[n][i, at(y), :].astype(F32) + rb[n][0, i].astype(F32) + rb[n][1, i].astype(F32)
                q[n][i] = total.astype(BF)
        elif stage == 2:
            for way, (which, lo) in enumerate(((zp, 0), (zm, half))):
                total = q[n][which, lo : lo + half, :].astype(F32) + sa[n][way].astype(F32)
                q[n][which, lo : lo + half, :] = total.astype(BF)
        else:
            _, cols = SHARD[n]
            for tile in range(cols // 128):
                at_cols = slice(tile * 128, (tile + 1) * 128)
                keep = mask_at(n, tile).astype(F32) * SCALE
                total = q[n][zh, :, at_cols].astype(F32) + sb[n][0, :, at_cols].astype(F32) + sb[n][1, :, at_cols].astype(F32)
                grads[n][:, at_cols] = total * keep

    def rs_step(n, stage):
        rs_wait(n, stage)
        rs_add(n, stage)
        if stage < 3:
            rs_start(n, stage + 1)

    def columns(n, k):
        part = w[n][:, :, pl.ds(pl.multiple_of(k * 256, 256), 256)]
        return part.reshape(part.shape[0] * part.shape[1], 256)

    def whole(ref):
        return ref[...].reshape(HID, ref.shape[-1])

    def each(count, step):
        lax.fori_loop(0, count, lambda k, carry: (step(k), carry)[1], 0)

    mask_shard(0)
    mask_shard(3)
    pl.semaphore_wait(barrier, len(partners))
    for n in (0, 3):
        ag_start(n, "z1")
        ag_start(n, "y1", 0)
    mask_shard(1)
    mask_shard(2)
    for copy in loads:
        copy.wait()
    tok_t[...] = tok[...].T
    for n in (0, 3):
        ag_wait(n, "z1")
        ag_start(n, "z2")
        ag_start(n, "y1", 1, 2)
    ag_start(1, "z1")
    ag_pass(0, 0)
    ag_wait(0, "z2")
    ag_start(0, "y1", 3)
    ag_start(2, "z1")
    ag_pass(0, 1, 2)
    ag_pass(3, 0)
    ag_wait(3, "z2")
    ag_start(3, "y1", 3)
    ag_pass(0, 3)
    ag_pass(3, 1, 2)
    ag_wait(0, "y2", 0, 1, 2, 3)

    def first(k):
        h[0][k] = dot(columns(0, k), tok_t[...], 0, 0).astype(BF)

    def back_first(k):
        h[1][k] = dot(w[3][k], cot[...], 1, 1).astype(BF)

    def inner(k):
        v = dot(columns(1, k), whole(u[0]), 0, 0)
        vv = v * v
        tanh = jnp.tanh(GELU_A * (v + GELU_B * (vv * v)))
        up = 0.5 * (1.0 + tanh)
        act[k] = (v * up).astype(BF)
        slope[k] = up + 0.5 * v * (1.0 - tanh * tanh) * (GELU_A * (1.0 + (3.0 * GELU_B) * vv))

    def lowered(k):
        h[2][k] = dot(columns(2, k), whole(act), 0, 0).astype(BF)

    def d_inner(k):
        d_in[k] = (dot(w[2][k], whole(u[1]), 1, 0) * slope[k]).astype(BF)

    def d_moved(k):
        h[3][k] = dot(w[1][k], whole(d_in), 1, 0).astype(BF)

    def mix(k):
        cols = pl.ds(pl.multiple_of(k * 256, 256), 256)
        part = u[2][:, :, cols].reshape(HID, 256)
        mixed[cols, :] = dot(part, whole(w[3]), 0, 0).astype(BF)

    def tok_grad(k):
        part = dot(w[0][k], whole(u[3]), 1, 0)
        tokens_grad[:, pl.ds(pl.multiple_of(k * 128, 128), 128)] = part.T.astype(BF)

    def grad_r_up(k):
        rows = pl.ds(pl.multiple_of(k * 128, 128), 128)
        p[0][k] = dot(tok_t[rows, :], whole(u[3]), 1, 1).astype(BF)

    def grad_l_up(k):
        p[1][k] = dot(u[0][k], whole(d_in), 1, 1).astype(BF)

    def grad_r_down(k):
        p[2][k] = dot(act[k], whole(u[1]), 1, 1).astype(BF)

    def grad_l_down(k):
        p[3][k] = dot(u[2][k], cot[...], 1, 0).astype(BF)

    def a_step(n, k):
        a_wait(n, k)
        if k:
            b_start(n, k)

    each(4, first)
    own_chunks(0)
    a_start(0, 2)
    a_start(0, 1)
    ag_pass(3, 3)
    ag_wait(1, "z1")
    ag_start(1, "z2")
    ag_start(1, "y1", 0, 1, 2)
    ag_wait(2, "z1")
    ag_start(2, "z2")
    ag_wait(3, "y2", 0, 1, 2, 3)
    each(4, back_first)
    own_chunks(1)
    a_step(0, 2)
    a_start(0, 3)
    ag_wait(1, "z2")
    ag_start(1, "y1", 3)
    a_step(0, 1)
    a_start(0, 0)
    ag_pass(1, 0)
    ag_wait(2, "z2")
    ag_start(2, "y1", 0, 1, 2, 3)
    ag_pass(1, 1, 2)
    a_step(0, 3)
    a_start(1, 2)
    ag_pass(1, 3)
    a_step(0, 0)
    a_start(1, 1)
    ag_pass(2, 0)
    a_step(1, 2)
    a_start(1, 3)
    ag_pass(2, 1, 2)
    a_step(1, 1)
    a_start(1, 0)
    ag_pass(2, 3)

    for k in (2, 1, 3):
        b_wait(0, k)
    ag_wait(1, "y2", 0, 1, 2, 3)
    each(4, inner)
    a_step(1, 3)
    ag_wait(2, "y2", 0, 1, 2, 3)
    each(4, lowered)
    own_chunks(2)
    a_start(2, 2)
    a_start(2, 1)
    a_step(1, 0)
    for k in (2, 1, 3):
        b_wait(1, k)
    each(4, grad_r_down)
    rs_start(2, 0)
    a_step(2, 2)
    a_start(2, 3)
    each(4, d_inner)
    a_step(2, 1)
    a_start(2, 0)
    each(4, d_moved)
    own_chunks(3)
    a_start(3, 2)
    rs_step(2, 0)
    a_step(2, 3)
    a_start(3, 1)
    each(4, grad_l_up)
    rs_start(1, 0)
    a_step(2, 0)
    a_start(3, 3)
    a_step(3, 2)
    a_start(3, 0)

    for k in (2, 1, 3):
        b_wait(2, k)
    each(4, grad_l_down)
    rs_start(3, 0)
    a_step(3, 1)
    rs_step(1, 0)
    rs_step(2, 1)
    a_step(3, 3)
    each(3, mix)
    rs_step(3, 0)
    a_step(3, 0)
    for k in (2, 1, 3):
        b_wait(3, k)
    each(4, grad_r_up)
    rs_start(0, 0)
    rs_step(2, 2)
    each(4, tok_grad)
    rs_step(1, 1)
    rs_step(0, 0)
    rs_step(3, 1)
    rs_step(1, 2)
    rs_step(0, 1)
    rs_step(3, 2)
    rs_step(2, 3)
    rs_step(1, 3)
    rs_step(0, 2)
    rs_step(3, 3)
    rs_step(0, 3)
    for copy in sent:
        copy.wait_send()


def write_kernel(*refs):
    results, places, held, sem = refs[:6], refs[6:12], refs[12:18], refs[18]
    ins = [pltpu.make_async_copy(a, b, sem.at[0, i]) for i, (a, b) in enumerate(zip(results, held))]
    outs = [pltpu.make_async_copy(a, b, sem.at[1, i]) for i, (a, b) in enumerate(zip(held, places))]
    for copy in ins:
        copy.start()
    for arrived, copy in zip(ins, outs):
        arrived.wait()
        copy.start()
    for copy in outs:
        copy.wait()


def per_device(*args):
    vmem = pl.BlockSpec(memory_space=pltpu.VMEM)
    smem = pl.BlockSpec(memory_space=pltpu.SMEM)
    anywhere = pl.BlockSpec(memory_space=pl.ANY)
    hidden = [pltpu.VMEM((4, 256, TOK), BF)]
    full = [pltpu.VMEM((4, 4 * rows, cols), BF) for rows, cols in SHARD]
    scratch = (
        [pltpu.VMEM((TOK, WID), BF), pltpu.VMEM((WID, TOK), BF), pltpu.VMEM((TOK, WID), BF)]
        + full * 2
        + hidden * 13
        + [pltpu.VMEM((4, 256, TOK), F32)]
        + hidden
        + [pltpu.VMEM((2, 2, rows, cols), BF) for rows, cols in SHARD]
        + [pltpu.VMEM((2, 4, rows, cols), BF) for rows, cols in SHARD]
        + [pltpu.VMEM((4, rows, cols), BF) for rows, cols in SHARD]
        + [pltpu.VMEM((2, rows // 2, cols), BF) for rows, cols in SHARD]
        + [pltpu.VMEM((2, rows, cols), BF) for rows, cols in SHARD]
        + [pltpu.SemaphoreType.DMA((2,))]
        + [pltpu.SemaphoreType.DMA((4, 16))] * 2
        + [pltpu.SemaphoreType.DMA((4, 4, 3))] * 2
        + [pltpu.SemaphoreType.DMA((4, 3))] * 2
        + [pltpu.SemaphoreType.DMA((4, 4, 2))] * 2
    )
    outs = pl.pallas_call(
        block_kernel,
        name="block",
        out_shape=(
            jax.ShapeDtypeStruct((TOK, WID), BF),
            jax.ShapeDtypeStruct((TOK, WID), BF),
            *(jax.ShapeDtypeStruct(shape, F32) for shape in SHARD),
        ),
        in_specs=[anywhere] + [vmem] * 4 + [smem] * 4 + [anywhere],
        out_specs=(vmem,) * 6,
        scratch_shapes=scratch,
        compiler_params=pltpu.CompilerParams(
            collective_id=0, has_side_effects=True, vmem_limit_bytes=60 * 2**20
        ),
        cost_estimate=pl.CostEstimate(
            flops=15_000_000_000, bytes_accessed=8_000_000, transcendentals=800_000
        ),
    )(*args[:8], args[8].swapaxes(1, 2), args[9])
    outs = pl.pallas_call(
        write_kernel,
        name="write",
        out_shape=tuple(jax.ShapeDtypeStruct(o.shape, o.dtype) for o in outs),
        in_specs=[anywhere] * 6,
        out_specs=(anywhere,) * 6,
        scratch_shapes=[pltpu.VMEM(o.shape, o.dtype) for o in outs] + [pltpu.SemaphoreType.DMA((2, 6))],
        cost_estimate=pl.CostEstimate(flops=0, bytes_accessed=5_000_000, transcendentals=0),
    )(*outs)
    return (outs[0], outs[1], *(g[None] for g in outs[2:]))


def solution(mesh):
    weight = P("tensor", "dp", None)
    mask = P("tensor", None, None)
    act = P("dp", "tensor")
    return jax.shard_map(
        per_device,
        mesh=mesh,
        in_specs=(act, weight, weight, weight, weight, mask, mask, mask, mask, act),
        out_specs=(act, act, weight, weight, weight, weight),
        check_vma=False,
    )
```

```python
import math

import jax
import jax.numpy as jnp
from jax import lax
from jax.experimental import pallas as pl
from jax.experimental.pallas import tpu as pltpu
from jax.sharding import PartitionSpec as P

MESH = pl.DeviceIdType.MESH
BF = jnp.bfloat16
F32 = jnp.float32
TOK = 768
HID = 1024
WID = 512
GELU_A = math.sqrt(2.0 / math.pi)
GELU_B = 0.044715
SCALE = 1.0 / math.sqrt(12288.0)
SHARD = ((32, 1024), (64, 1024), (64, 1024), (64, 512))


def dot(a, b, ca, cb):
    return lax.dot_general(a, b, (((ca,), (cb,)), ((), ())), preferred_element_type=F32)


def block_kernel(
    tok_hbm,
    r_up_hbm,
    l_up_hbm,
    r_down_hbm,
    l_down_hbm,
    m_r_up,
    m_l_up,
    m_r_down,
    m_l_down,
    cot_hbm,
    mixed_hbm,
    tokens_grad_hbm,
    g_r_up_hbm,
    g_l_up_hbm,
    g_r_down_hbm,
    g_l_down_hbm,
    tok,
    tok_t,
    cot,
    w_0,
    w_1,
    w_2,
    w_3,
    p_0,
    p_1,
    p_2,
    p_3,
    h_0,
    h_1,
    h_2,
    h_3,
    st_0,
    st_1,
    st_2,
    st_3,
    u_0,
    u_1,
    u_2,
    u_3,
    act,
    slope,
    d_in,
    ra_0,
    ra_1,
    ra_2,
    ra_3,
    rb_0,
    rb_1,
    rb_2,
    rb_3,
    q_0,
    q_1,
    q_2,
    q_3,
    sa_0,
    sa_1,
    sa_2,
    sa_3,
    sb_0,
    sb_1,
    sb_2,
    sb_3,
    load_sem,
    ag_send,
    ag_recv,
    a_send,
    a_recv,
    b_send,
    b_recv,
    rs_send,
    rs_recv,
    s_r_up,
    s_l_up,
    s_r_down,
    s_l_down,
    mixed,
    tokens_grad,
    g_r_up,
    g_l_up,
    g_r_down,
    g_l_down,
    shard_sem,
    out_sem,
):
    shards = (s_r_up, s_l_up, s_r_down, s_l_down)
    masks = (m_r_up, m_l_up, m_r_down, m_l_down)
    grads = (g_r_up, g_l_up, g_r_down, g_l_down)
    w = (w_0, w_1, w_2, w_3)
    p = (p_0, p_1, p_2, p_3)
    h = (h_0, h_1, h_2, h_3)
    st = (st_0, st_1, st_2, st_3)
    u = (u_0, u_1, u_2, u_3)
    ra = (ra_0, ra_1, ra_2, ra_3)
    rb = (rb_0, rb_1, rb_2, rb_3)
    q = (q_0, q_1, q_2, q_3)
    sa = (sa_0, sa_1, sa_2, sa_3)
    sb = (sb_0, sb_1, sb_2, sb_3)

    d = lax.axis_index("dp")
    t = lax.axis_index("tensor")
    zh, y = d // 4, d % 4
    x, j = t // 4, t % 4
    zl, c = j // 2, j % 2
    zp, zm = (zh + 1) % 4, (zh + 3) % 4
    yp, ym = (y + 1) % 4, (y + 3) % 4
    zo, yo = (zh + 2) % 4, (y + 2) % 4
    z_dev = ((zp * 4 + y, t), (zm * 4 + y, t))
    y_dev = ((zh * 4 + yp, t), (zh * 4 + ym, t))
    js = [j] + [((zl + i // 2) % 2) * 2 + (c + i % 2) % 2 for i in (1, 2, 3)]
    j_dev = [None] + [(d, x * 4 + js[i]) for i in (1, 2, 3)]
    xs = [(x + k) % 4 for k in range(4)]
    x_dev = [None] + [(d, xs[k] * 4 + j) for k in (1, 2, 3)]

    loads = [
        pltpu.make_async_copy(tok_hbm, tok, load_sem.at[0]),
        pltpu.make_async_copy(cot_hbm, cot, load_sem.at[1]),
    ]
    shard_loads = [
        pltpu.make_async_copy(src, dst, shard_sem.at[n])
        for n, (src, dst) in enumerate(zip((r_up_hbm, l_up_hbm, r_down_hbm, l_down_hbm), shards))
    ]
    for n in (0, 3, 1, 2):
        shard_loads[n].start()
    stores = [
        pltpu.make_async_copy(src, dst, out_sem.at[n])
        for n, (src, dst) in enumerate(
            (
                (mixed, mixed_hbm),
                (tokens_grad, tokens_grad_hbm),
                (g_r_up, g_r_up_hbm),
                (g_l_up, g_l_up_hbm),
                (g_r_down, g_r_down_hbm),
                (g_l_down, g_l_down_hbm),
            )
        )
    ]

    barrier = pltpu.get_barrier_semaphore()
    partners = list(z_dev) + list(y_dev) + j_dev[1:] + x_dev[1:]
    for device in partners:
        pl.semaphore_signal(barrier, inc=1, device_id=device, device_id_type=MESH)
    for copy in loads:
        copy.start()

    sent = []

    def remote(src, dst, send, recv, device):
        return pltpu.make_async_remote_copy(
            src_ref=src,
            dst_ref=dst,
            send_sem=send,
            recv_sem=recv,
            device_id=device,
            device_id_type=MESH,
        )

    def start(src, dst, send, recv, device):
        copy = remote(src, dst, send, recv, device)
        copy.start()
        sent.append(copy)

    def tile_row(n):
        return (d * SHARD[n][0]) // 128

    def mask_at(n, tile):
        if n == 3:
            return masks[n][0, tile, tile_row(n)]
        return masks[n][0, tile_row(n), tile]

    def mask_shard(n):
        rows, cols = SHARD[n]
        shard_loads[n].wait()
        for tile in range(cols // 128):
            keep = mask_at(n, tile).astype(F32)
            part = shards[n][0, :, tile * 128 : (tile + 1) * 128].astype(F32) * keep
            w[n][zh, pl.ds(pl.multiple_of(y * rows, rows), rows), tile * 128 : (tile + 1) * 128] = part.astype(BF)

    def at_y(ref, n, lead, which, lo=0, size=None):
        rows = SHARD[n][0]
        size = rows if size is None else size
        return ref.at[lead, pl.ds(pl.multiple_of(which * rows + lo, 16), size), :]

    near = (zh, zm, zp, zo)

    def ag_moves(n, stage, r=0):
        half = SHARD[n][0] // 2

        def at(lead, which, *part):
            return at_y(w[n], n, lead, which, *part)

        if stage == "z1":
            mine = at(zh, y)
            return ((mine, at(zm, y), 0, z_dev[0]), (mine, at(zp, y), 1, z_dev[1]))
        if stage == "z2":
            return (
                (at(zm, y, 0, half), at(zo, y, 0, half), 2, z_dev[0]),
                (at(zp, y, half, half), at(zo, y, half, half), 3, z_dev[1]),
            )
        lead = near[r]
        if stage == "y1":
            mine = at(lead, y)
            return ((mine, at(lead, ym), 4 + 2 * r, y_dev[0]), (mine, at(lead, yp), 5 + 2 * r, y_dev[1]))
        way = r % 2
        return ((at(lead, (ym, yp)[way]), at(lead, yo), 12 + r, y_dev[way]),)

    def ag_start(n, stage, *places):
        for r in places or (0,):
            for src, _, sem, device in ag_moves(n, stage, r):
                start(src, src, ag_send.at[n, sem], ag_recv.at[n, sem], device)

    def ag_wait(n, stage, *places):
        for r in places or (0,):
            for _, dst, sem, device in ag_moves(n, stage, r):
                remote(dst, dst, ag_send.at[n, sem], ag_recv.at[n, sem], device).wait_recv()

    def ag_pass(n, *places):
        for r in places:
            ag_wait(n, "y1", r)
            ag_start(n, "y2", r)

    def chunk(ref, lead, which):
        return ref.at[lead, pl.ds(pl.multiple_of(which * 64, 64), 64), :]

    def a_start(n, k):
        lead = xs[k]
        for i in (1, 2, 3):
            dst = chunk(u[n], x, j) if k == 0 else chunk(st[n], lead, j)
            start(chunk(h[n], lead, js[i]), dst, a_send.at[n, k, i - 1], a_recv.at[n, k, i - 1], j_dev[i])

    def a_wait(n, k):
        lead = xs[k]
        for i in (1, 2, 3):
            dst = chunk(u[n], x, js[i]) if k == 0 else chunk(st[n], lead, js[i])
            remote(dst, dst, a_send.at[n, k, i - 1], a_recv.at[n, k, i - 1], j_dev[i]).wait_recv()

    def own_chunks(n):
        for k in range(4):
            dst = u[n] if k == 0 else st[n]
            rows = pl.ds(pl.multiple_of(j * 64, 64), 64)
            dst[xs[k], rows, :] = h[n][xs[k], rows, :]

    def b_start(n, k):
        start(st[n].at[xs[k]], u[n].at[x], b_send.at[n, k - 1], b_recv.at[n, k - 1], x_dev[k])

    def b_wait(n, k):
        dst = u[n].at[xs[4 - k]]
        remote(dst, dst, b_send.at[n, k - 1], b_recv.at[n, k - 1], x_dev[k]).wait_recv()

    def rs_places(n, stage):
        half = SHARD[n][0] // 2
        if stage == 0:
            return (
                (at_y(p[n], n, pl.ds(0, 2), yo), at_y(p[n], n, pl.ds(2, 2), yo)),
                (ra[n].at[0, pl.ds(0, 2)], ra[n].at[1, pl.ds(0, 2)]),
            )
        if stage == 1:
            return (
                (at_y(p[n], n, pl.ds(0, 4), yp), at_y(p[n], n, pl.ds(0, 4), ym)),
                (rb[n].at[0], rb[n].at[1]),
            )
        if stage == 2:
            return (
                (q[n].at[zo, pl.ds(0, half)], q[n].at[zo, pl.ds(half, half)]),
                (sa[n].at[0], sa[n].at[1]),
            )
        return (q[n].at[zp], q[n].at[zm]), (sb[n].at[0], sb[n].at[1])

    def rs_start(n, stage):
        out, into = rs_places(n, stage)
        devices = y_dev if stage < 2 else z_dev
        for way in (0, 1):
            start(out[way], into[way], rs_send.at[n, stage, way], rs_recv.at[n, stage, way], devices[way])

    def rs_wait(n, stage):
        _, into = rs_places(n, stage)
        devices = y_dev if stage < 2 else z_dev
        for way in (0, 1):
            remote(into[way], into[way], rs_send.at[n, stage, way], rs_recv.at[n, stage, way], devices[way]).wait_recv()

    def rs_add(n, stage):
        rows, _ = SHARD[n]
        half = rows // 2

        def at(which):
            return pl.ds(pl.multiple_of(which * rows, rows), rows)

        if stage == 0:
            for way, (lead, which) in enumerate(((0, yp), (2, ym))):
                for i in (0, 1):
                    total = p[n][lead + i, at(which), :].astype(F32) + ra[n][way, i].astype(F32)
                    p[n][lead + i, at(which), :] = total.astype(BF)
        elif stage == 1:
            for i in range(4):
                total = p[n][i, at(y), :].astype(F32) + rb[n][0, i].astype(F32) + rb[n][1, i].astype(F32)
                q[n][i] = total.astype(BF)
        elif stage == 2:
            for way, (which, lo) in enumerate(((zp, 0), (zm, half))):
                total = q[n][which, lo : lo + half, :].astype(F32) + sa[n][way].astype(F32)
                q[n][which, lo : lo + half, :] = total.astype(BF)
        else:
            _, cols = SHARD[n]
            for tile in range(cols // 128):
                at_cols = slice(tile * 128, (tile + 1) * 128)
                keep = mask_at(n, tile).astype(F32) * SCALE
                total = q[n][zh, :, at_cols].astype(F32) + sb[n][0, :, at_cols].astype(F32) + sb[n][1, :, at_cols].astype(F32)
                grads[n][:, at_cols] = total * keep

    def rs_step(n, stage):
        rs_wait(n, stage)
        rs_add(n, stage)
        if stage < 3:
            rs_start(n, stage + 1)

    def columns(n, k):
        part = w[n][:, :, pl.ds(pl.multiple_of(k * 256, 256), 256)]
        return part.reshape(part.shape[0] * part.shape[1], 256)

    def whole(ref):
        return ref[...].reshape(HID, ref.shape[-1])

    def each(count, step):
        lax.fori_loop(0, count, lambda k, carry: (step(k), carry)[1], 0)

    mask_shard(0)
    mask_shard(3)
    pl.semaphore_wait(barrier, len(partners))
    for n in (0, 3):
        ag_start(n, "z1")
        ag_start(n, "y1", 0)
    mask_shard(1)
    mask_shard(2)
    for copy in loads:
        copy.wait()
    tok_t[...] = tok[...].T
    for n in (0, 3):
        ag_wait(n, "z1")
        ag_start(n, "z2")
        ag_start(n, "y1", 1, 2)
    ag_pass(0, 0)
    ag_wait(0, "z2")
    ag_start(0, "y1", 3)
    ag_start(1, "z1")
    ag_pass(0, 1, 2)
    ag_pass(3, 0)
    ag_wait(3, "z2")
    ag_start(3, "y1", 3)
    ag_start(2, "z1")
    ag_pass(0, 3)
    ag_pass(3, 1, 2)
    ag_wait(0, "y2", 0, 1, 2, 3)

    def first(k):
        h[0][k] = dot(columns(0, k), tok_t[...], 0, 0).astype(BF)

    def back_first(k):
        h[1][k] = dot(w[3][k], cot[...], 1, 1).astype(BF)

    def inner(k):
        v = dot(columns(1, k), whole(u[0]), 0, 0)
        vv = v * v
        tanh = jnp.tanh(GELU_A * (v + GELU_B * (vv * v)))
        up = 0.5 * (1.0 + tanh)
        act[k] = (v * up).astype(BF)
        slope[k] = up + 0.5 * v * (1.0 - tanh * tanh) * (GELU_A * (1.0 + (3.0 * GELU_B) * vv))

    def lowered(k):
        h[2][k] = dot(columns(2, k), whole(act), 0, 0).astype(BF)

    def d_inner(k):
        d_in[k] = (dot(w[2][k], whole(u[1]), 1, 0) * slope[k]).astype(BF)

    def d_moved(k):
        h[3][k] = dot(w[1][k], whole(d_in), 1, 0).astype(BF)

    def mix(k):
        cols = pl.ds(pl.multiple_of(k * 256, 256), 256)
        part = u[2][:, :, cols].reshape(HID, 256)
        mixed[cols, :] = dot(part, whole(w[3]), 0, 0).astype(BF)

    def tok_grad(k):
        part = dot(w[0][k], whole(u[3]), 1, 0)
        tokens_grad[:, pl.ds(pl.multiple_of(k * 128, 128), 128)] = part.T.astype(BF)

    def grad_r_up(k):
        rows = pl.ds(pl.multiple_of(k * 128, 128), 128)
        p[0][k] = dot(tok_t[rows, :], whole(u[3]), 1, 1).astype(BF)

    def grad_l_up(k):
        p[1][k] = dot(u[0][k], whole(d_in), 1, 1).astype(BF)

    def grad_r_down(k):
        p[2][k] = dot(act[k], whole(u[1]), 1, 1).astype(BF)

    def grad_l_down(k):
        p[3][k] = dot(u[2][k], cot[...], 1, 0).astype(BF)

    def a_step(n, k):
        a_wait(n, k)
        if k:
            b_start(n, k)

    each(4, first)
    own_chunks(0)
    a_start(0, 2)
    a_start(0, 1)
    ag_pass(3, 3)
    ag_wait(1, "z1")
    ag_start(1, "z2")
    ag_start(1, "y1", 0, 1, 2)
    ag_wait(2, "z1")
    ag_start(2, "z2")
    ag_wait(3, "y2", 0, 1, 2, 3)
    each(4, back_first)
    own_chunks(1)
    ag_pass(1, 0)
    ag_start(2, "y1", 0)
    a_step(0, 2)
    a_start(0, 3)
    ag_wait(1, "z2")
    ag_start(1, "y1", 3)
    ag_pass(1, 1, 2)
    ag_start(2, "y1", 1, 2)
    a_step(0, 1)
    a_start(0, 0)
    ag_wait(2, "z2")
    ag_start(2, "y1", 3)
    ag_pass(1, 3)
    a_step(0, 3)
    a_start(1, 2)
    ag_pass(2, 0)
    a_step(0, 0)
    a_start(1, 1)
    ag_pass(2, 1, 2)
    a_step(1, 2)
    a_start(1, 3)
    a_step(1, 1)
    a_start(1, 0)
    ag_pass(2, 3)

    for k in (2, 1, 3):
        b_wait(0, k)
    ag_wait(1, "y2", 0, 1, 2, 3)
    each(4, inner)
    a_step(1, 3)
    ag_wait(2, "y2", 0, 1, 2, 3)
    each(4, lowered)
    own_chunks(2)
    a_start(2, 2)
    a_start(2, 1)
    a_step(1, 0)
    for k in (2, 1, 3):
        b_wait(1, k)
    each(4, grad_r_down)
    rs_start(2, 0)
    a_step(2, 2)
    a_start(2, 3)
    each(4, d_inner)
    a_step(2, 1)
    a_start(2, 0)
    each(4, d_moved)
    own_chunks(3)
    a_start(3, 2)
    rs_step(2, 0)
    a_step(2, 3)
    a_start(3, 1)
    each(4, grad_l_up)
    rs_start(1, 0)
    a_step(2, 0)
    a_start(3, 3)
    a_step(3, 2)
    a_start(3, 0)

    for k in (2, 1, 3):
        b_wait(2, k)
    each(4, grad_l_down)
    rs_start(3, 0)
    a_step(3, 1)
    rs_step(1, 0)
    rs_step(2, 1)
    a_step(3, 3)
    each(3, mix)
    stores[0].start()
    rs_step(3, 0)
    a_step(3, 0)
    for k in (2, 1, 3):
        b_wait(3, k)
    each(4, grad_r_up)
    rs_start(0, 0)
    rs_step(2, 2)
    each(4, tok_grad)
    stores[1].start()
    rs_step(1, 1)
    rs_step(0, 0)
    rs_step(3, 1)
    rs_step(1, 2)
    rs_step(0, 1)
    rs_step(3, 2)
    rs_step(2, 3)
    stores[4].start()
    rs_step(1, 3)
    stores[3].start()
    rs_step(0, 2)
    rs_step(3, 3)
    stores[5].start()
    rs_step(0, 3)
    stores[2].start()
    for copy in stores:
        copy.wait()
    for copy in sent:
        copy.wait_send()


def write_kernel(*refs):
    results, places, held, sem = refs[:6], refs[6:12], refs[12:18], refs[18]
    ins = [pltpu.make_async_copy(a, b, sem.at[0, i]) for i, (a, b) in enumerate(zip(results, held))]
    outs = [pltpu.make_async_copy(a, b, sem.at[1, i]) for i, (a, b) in enumerate(zip(held, places))]
    for copy in ins:
        copy.start()
    for arrived, copy in zip(ins, outs):
        arrived.wait()
        copy.start()
    for copy in outs:
        copy.wait()


def per_device(*args):
    smem = pl.BlockSpec(memory_space=pltpu.SMEM)
    anywhere = pl.BlockSpec(memory_space=pl.ANY)
    hidden = [pltpu.VMEM((4, 256, TOK), BF)]
    full = [pltpu.VMEM((4, 4 * rows, cols), BF) for rows, cols in SHARD]
    scratch = (
        [pltpu.VMEM((TOK, WID), BF), pltpu.VMEM((WID, TOK), BF), pltpu.VMEM((TOK, WID), BF)]
        + full * 2
        + hidden * 13
        + [pltpu.VMEM((4, 256, TOK), F32)]
        + hidden
        + [pltpu.VMEM((2, 2, rows, cols), BF) for rows, cols in SHARD]
        + [pltpu.VMEM((2, 4, rows, cols), BF) for rows, cols in SHARD]
        + [pltpu.VMEM((4, rows, cols), BF) for rows, cols in SHARD]
        + [pltpu.VMEM((2, rows // 2, cols), BF) for rows, cols in SHARD]
        + [pltpu.VMEM((2, rows, cols), BF) for rows, cols in SHARD]
        + [pltpu.SemaphoreType.DMA((2,))]
        + [pltpu.SemaphoreType.DMA((4, 16))] * 2
        + [pltpu.SemaphoreType.DMA((4, 4, 3))] * 2
        + [pltpu.SemaphoreType.DMA((4, 3))] * 2
        + [pltpu.SemaphoreType.DMA((4, 4, 2))] * 2
        + [pltpu.VMEM((1, rows, cols), BF) for rows, cols in SHARD]
        + [pltpu.VMEM((TOK, WID), BF)] * 2
        + [pltpu.VMEM(shape, F32) for shape in SHARD]
        + [pltpu.SemaphoreType.DMA((4,)), pltpu.SemaphoreType.DMA((6,))]
    )
    outs = pl.pallas_call(
        block_kernel,
        name="block",
        out_shape=(
            jax.ShapeDtypeStruct((TOK, WID), BF),
            jax.ShapeDtypeStruct((TOK, WID), BF),
            *(jax.ShapeDtypeStruct(shape, F32) for shape in SHARD),
        ),
        in_specs=[anywhere] * 5 + [smem] * 4 + [anywhere],
        out_specs=(anywhere,) * 6,
        scratch_shapes=scratch,
        compiler_params=pltpu.CompilerParams(
            collective_id=0, has_side_effects=True, vmem_limit_bytes=60 * 2**20
        ),
        cost_estimate=pl.CostEstimate(
            flops=15_000_000_000, bytes_accessed=8_000_000, transcendentals=800_000
        ),
    )(*args[:8], args[8].swapaxes(1, 2), args[9])
    outs = pl.pallas_call(
        write_kernel,
        name="write",
        out_shape=tuple(jax.ShapeDtypeStruct(o.shape, o.dtype) for o in outs),
        in_specs=[anywhere] * 6,
        out_specs=(anywhere,) * 6,
        scratch_shapes=[pltpu.VMEM(o.shape, o.dtype) for o in outs] + [pltpu.SemaphoreType.DMA((2, 6))],
        cost_estimate=pl.CostEstimate(flops=0, bytes_accessed=5_000_000, transcendentals=0),
    )(*outs)
    return (outs[0], outs[1], *(g[None] for g in outs[2:]))


def solution(mesh):
    weight = P("tensor", "dp", None)
    mask = P("tensor", None, None)
    act = P("dp", "tensor")
    return jax.shard_map(
        per_device,
        mesh=mesh,
        in_specs=(act, weight, weight, weight, weight, mask, mask, mask, mask, act),
        out_specs=(act, act, weight, weight, weight, weight),
        check_vma=False,
    )
```

```python
import math

import jax
import jax.numpy as jnp
from jax import lax
from jax.experimental import pallas as pl
from jax.experimental.pallas import tpu as pltpu
from jax.sharding import PartitionSpec as P

MESH = pl.DeviceIdType.MESH
BF = jnp.bfloat16
F32 = jnp.float32
TOK = 768
HID = 1024
WID = 512
GELU_A = math.sqrt(2.0 / math.pi)
GELU_B = 0.044715
SCALE = 1.0 / math.sqrt(12288.0)
SHARD = ((32, 1024), (64, 1024), (64, 1024), (64, 512))


def dot(a, b, ca, cb):
    return lax.dot_general(a, b, (((ca,), (cb,)), ((), ())), preferred_element_type=F32)


def block_kernel(
    tok_hbm,
    r_up_hbm,
    l_up_hbm,
    r_down_hbm,
    l_down_hbm,
    m_r_up,
    m_l_up,
    m_r_down,
    m_l_down,
    cot_hbm,
    mixed_hbm,
    tokens_grad_hbm,
    g_r_up_hbm,
    g_l_up_hbm,
    g_r_down_hbm,
    g_l_down_hbm,
    tok,
    tok_t,
    cot,
    w_0,
    w_1,
    w_2,
    w_3,
    p_0,
    p_1,
    p_2,
    p_3,
    h_0,
    h_1,
    h_2,
    h_3,
    st_0,
    st_1,
    st_2,
    st_3,
    u_0,
    u_1,
    u_2,
    u_3,
    act,
    slope,
    d_in,
    ra_0,
    ra_1,
    ra_2,
    ra_3,
    rb_0,
    rb_1,
    rb_2,
    rb_3,
    q_0,
    q_1,
    q_2,
    q_3,
    sa_0,
    sa_1,
    sa_2,
    sa_3,
    sb_0,
    sb_1,
    sb_2,
    sb_3,
    load_sem,
    ag_send,
    ag_recv,
    a_send,
    a_recv,
    b_send,
    b_recv,
    rs_send,
    rs_recv,
    s_r_up,
    s_l_up,
    s_r_down,
    s_l_down,
    mixed,
    tokens_grad,
    g_r_up,
    g_l_up,
    g_r_down,
    g_l_down,
    shard_sem,
    out_sem,
):
    shards = (s_r_up, s_l_up, s_r_down, s_l_down)
    masks = (m_r_up, m_l_up, m_r_down, m_l_down)
    grads = (g_r_up, g_l_up, g_r_down, g_l_down)
    w = (w_0, w_1, w_2, w_3)
    p = (p_0, p_1, p_2, p_3)
    h = (h_0, h_1, h_2, h_3)
    st = (st_0, st_1, st_2, st_3)
    u = (u_0, u_1, u_2, u_3)
    ra = (ra_0, ra_1, ra_2, ra_3)
    rb = (rb_0, rb_1, rb_2, rb_3)
    q = (q_0, q_1, q_2, q_3)
    sa = (sa_0, sa_1, sa_2, sa_3)
    sb = (sb_0, sb_1, sb_2, sb_3)

    d = lax.axis_index("dp")
    t = lax.axis_index("tensor")
    zh, y = d // 4, d % 4
    x, j = t // 4, t % 4
    zl, c = j // 2, j % 2
    zp, zm = (zh + 1) % 4, (zh + 3) % 4
    yp, ym = (y + 1) % 4, (y + 3) % 4
    zo, yo = (zh + 2) % 4, (y + 2) % 4
    z_dev = ((zp * 4 + y, t), (zm * 4 + y, t))
    y_dev = ((zh * 4 + yp, t), (zh * 4 + ym, t))
    js = [j] + [((zl + i // 2) % 2) * 2 + (c + i % 2) % 2 for i in (1, 2, 3)]
    j_dev = [None] + [(d, x * 4 + js[i]) for i in (1, 2, 3)]
    xs = [(x + k) % 4 for k in range(4)]
    x_dev = [None] + [(d, xs[k] * 4 + j) for k in (1, 2, 3)]

    loads = [
        pltpu.make_async_copy(tok_hbm, tok, load_sem.at[0]),
        pltpu.make_async_copy(cot_hbm, cot, load_sem.at[1]),
    ]
    shard_loads = [
        pltpu.make_async_copy(src, dst, shard_sem.at[n])
        for n, (src, dst) in enumerate(zip((r_up_hbm, l_up_hbm, r_down_hbm, l_down_hbm), shards))
    ]
    for n in (0, 3, 1, 2):
        shard_loads[n].start()
    stores = [
        pltpu.make_async_copy(src, dst, out_sem.at[n])
        for n, (src, dst) in enumerate(
            (
                (mixed, mixed_hbm),
                (tokens_grad, tokens_grad_hbm),
                (g_r_up, g_r_up_hbm),
                (g_l_up, g_l_up_hbm),
                (g_r_down, g_r_down_hbm),
                (g_l_down, g_l_down_hbm),
            )
        )
    ]

    barrier = pltpu.get_barrier_semaphore()
    partners = list(z_dev) + list(y_dev) + j_dev[1:] + x_dev[1:]
    for device in partners:
        pl.semaphore_signal(barrier, inc=1, device_id=device, device_id_type=MESH)
    for copy in loads:
        copy.start()

    sent = []

    def remote(src, dst, send, recv, device):
        return pltpu.make_async_remote_copy(
            src_ref=src,
            dst_ref=dst,
            send_sem=send,
            recv_sem=recv,
            device_id=device,
            device_id_type=MESH,
        )

    def start(src, dst, send, recv, device):
        copy = remote(src, dst, send, recv, device)
        copy.start()
        sent.append(copy)

    def tile_row(n):
        return (d * SHARD[n][0]) // 128

    def mask_at(n, tile):
        if n == 3:
            return masks[n][0, tile, tile_row(n)]
        return masks[n][0, tile_row(n), tile]

    def mask_shard(n):
        rows, cols = SHARD[n]
        shard_loads[n].wait()
        for tile in range(cols // 128):
            keep = mask_at(n, tile).astype(F32)
            part = shards[n][0, :, tile * 128 : (tile + 1) * 128].astype(F32) * keep
            w[n][zh, pl.ds(pl.multiple_of(y * rows, rows), rows), tile * 128 : (tile + 1) * 128] = part.astype(BF)

    def at_y(ref, n, lead, which, lo=0, size=None):
        rows = SHARD[n][0]
        size = rows if size is None else size
        return ref.at[lead, pl.ds(pl.multiple_of(which * rows + lo, 16), size), :]

    near = (zh, zm, zp, zo)

    def ag_moves(n, stage, r=0):
        half = SHARD[n][0] // 2

        def at(lead, which, *part):
            return at_y(w[n], n, lead, which, *part)

        if stage == "z1":
            mine = at(zh, y)
            return ((mine, at(zm, y), 0, z_dev[0]), (mine, at(zp, y), 1, z_dev[1]))
        if stage == "z2":
            return (
                (at(zm, y, 0, half), at(zo, y, 0, half), 2, z_dev[0]),
                (at(zp, y, half, half), at(zo, y, half, half), 3, z_dev[1]),
            )
        lead = near[r]
        if stage == "y1":
            mine = at(lead, y)
            return ((mine, at(lead, ym), 4 + 2 * r, y_dev[0]), (mine, at(lead, yp), 5 + 2 * r, y_dev[1]))
        way = r % 2
        return ((at(lead, (ym, yp)[way]), at(lead, yo), 12 + r, y_dev[way]),)

    def ag_start(n, stage, *places):
        for r in places or (0,):
            for src, _, sem, device in ag_moves(n, stage, r):
                start(src, src, ag_send.at[n, sem], ag_recv.at[n, sem], device)

    def ag_wait(n, stage, *places):
        for r in places or (0,):
            for _, dst, sem, device in ag_moves(n, stage, r):
                remote(dst, dst, ag_send.at[n, sem], ag_recv.at[n, sem], device).wait_recv()

    def ag_pass(n, *places):
        for r in places:
            ag_wait(n, "y1", r)
            ag_start(n, "y2", r)

    def chunk(ref, lead, which):
        return ref.at[lead, pl.ds(pl.multiple_of(which * 64, 64), 64), :]

    def a_start(n, k):
        lead = xs[k]
        for i in (1, 2, 3):
            dst = chunk(u[n], x, j) if k == 0 else chunk(st[n], lead, j)
            start(chunk(h[n], lead, js[i]), dst, a_send.at[n, k, i - 1], a_recv.at[n, k, i - 1], j_dev[i])

    def a_wait(n, k):
        lead = xs[k]
        for i in (1, 2, 3):
            dst = chunk(u[n], x, js[i]) if k == 0 else chunk(st[n], lead, js[i])
            remote(dst, dst, a_send.at[n, k, i - 1], a_recv.at[n, k, i - 1], j_dev[i]).wait_recv()

    def own_chunks(n):
        for k in range(4):
            dst = u[n] if k == 0 else st[n]
            rows = pl.ds(pl.multiple_of(j * 64, 64), 64)
            dst[xs[k], rows, :] = h[n][xs[k], rows, :]

    def b_start(n, k):
        start(st[n].at[xs[k]], u[n].at[x], b_send.at[n, k - 1], b_recv.at[n, k - 1], x_dev[k])

    def b_wait(n, k):
        dst = u[n].at[xs[4 - k]]
        remote(dst, dst, b_send.at[n, k - 1], b_recv.at[n, k - 1], x_dev[k]).wait_recv()

    def rs_places(n, stage):
        half = SHARD[n][0] // 2
        if stage == 0:
            return (
                (at_y(p[n], n, pl.ds(0, 2), yo), at_y(p[n], n, pl.ds(2, 2), yo)),
                (ra[n].at[0, pl.ds(0, 2)], ra[n].at[1, pl.ds(0, 2)]),
            )
        if stage == 1:
            return (
                (at_y(p[n], n, pl.ds(0, 4), yp), at_y(p[n], n, pl.ds(0, 4), ym)),
                (rb[n].at[0], rb[n].at[1]),
            )
        if stage == 2:
            return (
                (q[n].at[zo, pl.ds(0, half)], q[n].at[zo, pl.ds(half, half)]),
                (sa[n].at[0], sa[n].at[1]),
            )
        return (q[n].at[zp], q[n].at[zm]), (sb[n].at[0], sb[n].at[1])

    def rs_start(n, stage):
        out, into = rs_places(n, stage)
        devices = y_dev if stage < 2 else z_dev
        for way in (0, 1):
            start(out[way], into[way], rs_send.at[n, stage, way], rs_recv.at[n, stage, way], devices[way])

    def rs_wait(n, stage):
        _, into = rs_places(n, stage)
        devices = y_dev if stage < 2 else z_dev
        for way in (0, 1):
            remote(into[way], into[way], rs_send.at[n, stage, way], rs_recv.at[n, stage, way], devices[way]).wait_recv()

    def rs_add(n, stage):
        rows, _ = SHARD[n]
        half = rows // 2

        def at(which):
            return pl.ds(pl.multiple_of(which * rows, rows), rows)

        if stage == 0:
            for way, (lead, which) in enumerate(((0, yp), (2, ym))):
                for i in (0, 1):
                    total = p[n][lead + i, at(which), :].astype(F32) + ra[n][way, i].astype(F32)
                    p[n][lead + i, at(which), :] = total.astype(BF)
        elif stage == 1:
            for i in range(4):
                total = p[n][i, at(y), :].astype(F32) + rb[n][0, i].astype(F32) + rb[n][1, i].astype(F32)
                q[n][i] = total.astype(BF)
        elif stage == 2:
            for way, (which, lo) in enumerate(((zp, 0), (zm, half))):
                total = q[n][which, lo : lo + half, :].astype(F32) + sa[n][way].astype(F32)
                q[n][which, lo : lo + half, :] = total.astype(BF)
        else:
            _, cols = SHARD[n]
            for tile in range(cols // 128):
                at_cols = slice(tile * 128, (tile + 1) * 128)
                keep = mask_at(n, tile).astype(F32) * SCALE
                total = q[n][zh, :, at_cols].astype(F32) + sb[n][0, :, at_cols].astype(F32) + sb[n][1, :, at_cols].astype(F32)
                grads[n][:, at_cols] = total * keep

    def rs_step(n, stage):
        rs_wait(n, stage)
        rs_add(n, stage)
        if stage < 3:
            rs_start(n, stage + 1)

    def columns(n, k):
        part = w[n][:, :, pl.ds(pl.multiple_of(k * 256, 256), 256)]
        return part.reshape(part.shape[0] * part.shape[1], 256)

    def whole(ref):
        return ref[...].reshape(HID, ref.shape[-1])

    def each(count, step):
        lax.fori_loop(0, count, lambda k, carry: (step(k), carry)[1], 0)

    mask_shard(0)
    mask_shard(3)
    pl.semaphore_wait(barrier, len(partners))
    for n in (0, 3):
        ag_start(n, "z1")
        ag_start(n, "y1", 0)
    mask_shard(1)
    mask_shard(2)
    for copy in loads:
        copy.wait()
    tok_t[...] = tok[...].T
    for n in (0, 3):
        ag_wait(n, "z1")
        ag_start(n, "z2")
        ag_start(n, "y1", 1, 2)
    ag_pass(0, 0)
    ag_wait(0, "z2")
    ag_start(0, "y1", 3)
    ag_start(1, "z1")
    ag_pass(0, 1, 2)
    ag_pass(3, 0)
    ag_wait(3, "z2")
    ag_start(3, "y1", 3)
    ag_start(2, "z1")
    ag_pass(0, 3)
    ag_pass(3, 1, 2)
    ag_wait(0, "y2", 0, 1, 2, 3)

    def first(k):
        h[0][k] = dot(columns(0, k), tok_t[...], 0, 0).astype(BF)

    def back_first(k):
        h[1][k] = dot(w[3][k], cot[...], 1, 1).astype(BF)

    def inner(k):
        v = dot(columns(1, k), whole(u[0]), 0, 0)
        vv = v * v
        tanh = jnp.tanh(GELU_A * (v + GELU_B * (vv * v)))
        up = 0.5 * (1.0 + tanh)
        act[k] = (v * up).astype(BF)
        slope[k] = up + 0.5 * v * (1.0 - tanh * tanh) * (GELU_A * (1.0 + (3.0 * GELU_B) * vv))

    def lowered(k):
        h[2][k] = dot(columns(2, k), whole(act), 0, 0).astype(BF)

    def d_inner(k):
        d_in[k] = (dot(w[2][k], whole(u[1]), 1, 0) * slope[k]).astype(BF)

    def d_moved(k):
        h[3][k] = dot(w[1][k], whole(d_in), 1, 0).astype(BF)

    def mix(k):
        cols = pl.ds(pl.multiple_of(k * 256, 256), 256)
        part = u[2][:, :, cols].reshape(HID, 256)
        mixed[cols, :] = dot(part, whole(w[3]), 0, 0).astype(BF)

    def tok_grad(k):
        part = dot(w[0][k], whole(u[3]), 1, 0)
        tokens_grad[:, pl.ds(pl.multiple_of(k * 128, 128), 128)] = part.T.astype(BF)

    def grad_r_up(k):
        rows = pl.ds(pl.multiple_of(k * 128, 128), 128)
        p[0][k] = dot(tok_t[rows, :], whole(u[3]), 1, 1).astype(BF)

    def grad_l_up(k):
        p[1][k] = dot(u[0][k], whole(d_in), 1, 1).astype(BF)

    def grad_r_down(k):
        p[2][k] = dot(act[k], whole(u[1]), 1, 1).astype(BF)

    def grad_l_down(k):
        p[3][k] = dot(u[2][k], cot[...], 1, 0).astype(BF)

    def a_step(n, k):
        a_wait(n, k)
        if k:
            b_start(n, k)

    each(4, first)
    own_chunks(0)
    a_start(0, 2)
    a_start(0, 1)
    ag_pass(3, 3)
    ag_wait(1, "z1")
    ag_start(1, "z2")
    ag_start(1, "y1", 0, 1, 2)
    ag_wait(2, "z1")
    ag_start(2, "z2")
    ag_wait(3, "y2", 0, 1, 2, 3)
    each(4, back_first)
    own_chunks(1)
    ag_pass(1, 0)
    ag_start(2, "y1", 0)
    a_step(0, 2)
    a_start(0, 3)
    ag_wait(1, "z2")
    ag_start(1, "y1", 3)
    ag_pass(1, 1, 2)
    ag_start(2, "y1", 1, 2)
    a_step(0, 1)
    a_start(0, 0)
    ag_wait(2, "z2")
    ag_start(2, "y1", 3)
    ag_pass(1, 3)
    a_step(0, 3)
    a_start(1, 2)
    ag_pass(2, 0)
    a_step(0, 0)
    a_start(1, 1)
    ag_pass(2, 1, 2)
    a_step(1, 2)
    a_start(1, 3)
    a_step(1, 1)
    a_start(1, 0)
    ag_pass(2, 3)

    for k in (2, 1, 3):
        b_wait(0, k)
    ag_wait(1, "y2", 0, 1, 2, 3)
    each(4, inner)
    a_step(1, 3)
    ag_wait(2, "y2", 0, 1, 2, 3)
    each(4, lowered)
    own_chunks(2)
    a_start(2, 2)
    a_start(2, 1)
    a_step(1, 0)
    for k in (2, 1, 3):
        b_wait(1, k)
    each(4, grad_r_down)
    rs_start(2, 0)
    a_step(2, 2)
    a_start(2, 3)
    each(4, d_inner)
    a_step(2, 1)
    a_start(2, 0)
    each(4, d_moved)
    own_chunks(3)
    a_start(3, 2)
    rs_step(2, 0)
    a_step(2, 3)
    a_start(3, 1)
    each(4, grad_l_up)
    rs_start(1, 0)
    a_step(2, 0)
    a_start(3, 3)
    a_step(3, 2)
    a_start(3, 0)

    for k in (2, 1, 3):
        b_wait(2, k)
    each(4, grad_l_down)
    rs_start(3, 0)
    a_step(3, 1)
    rs_step(1, 0)
    a_step(3, 3)
    each(3, mix)
    stores[0].start()
    rs_step(3, 0)
    a_step(3, 0)
    rs_step(2, 1)
    for k in (2, 1, 3):
        b_wait(3, k)
    each(4, grad_r_up)
    rs_start(0, 0)
    rs_step(2, 2)
    each(4, tok_grad)
    stores[1].start()
    rs_step(1, 1)
    rs_step(0, 0)
    rs_step(3, 1)
    rs_step(1, 2)
    rs_step(0, 1)
    rs_step(3, 2)
    rs_step(2, 3)
    stores[4].start()
    rs_step(1, 3)
    stores[3].start()
    rs_step(0, 2)
    rs_step(3, 3)
    stores[5].start()
    rs_step(0, 3)
    stores[2].start()
    for copy in stores:
        copy.wait()
    for copy in sent:
        copy.wait_send()


def write_kernel(*refs):
    results, places, held, sem = refs[:6], refs[6:12], refs[12:18], refs[18]
    parts = []
    for i, ref in enumerate(held):
        rows = ref.shape[0]
        cut = 4 if rows == TOK else 1
        parts += [(i, pl.ds(at * (rows // cut), rows // cut)) for at in range(cut)]
    ins = [pltpu.make_async_copy(results[i].at[at], held[i].at[at], sem.at[0, n]) for n, (i, at) in enumerate(parts)]
    outs = [pltpu.make_async_copy(held[i].at[at], places[i].at[at], sem.at[1, n]) for n, (i, at) in enumerate(parts)]
    for copy in ins:
        copy.start()
    for arrived, copy in zip(ins, outs):
        arrived.wait()
        copy.start()
    for copy in outs:
        copy.wait()


def per_device(*args):
    smem = pl.BlockSpec(memory_space=pltpu.SMEM)
    anywhere = pl.BlockSpec(memory_space=pl.ANY)
    hidden = [pltpu.VMEM((4, 256, TOK), BF)]
    full = [pltpu.VMEM((4, 4 * rows, cols), BF) for rows, cols in SHARD]
    scratch = (
        [pltpu.VMEM((TOK, WID), BF), pltpu.VMEM((WID, TOK), BF), pltpu.VMEM((TOK, WID), BF)]
        + full * 2
        + hidden * 13
        + [pltpu.VMEM((4, 256, TOK), F32)]
        + hidden
        + [pltpu.VMEM((2, 2, rows, cols), BF) for rows, cols in SHARD]
        + [pltpu.VMEM((2, 4, rows, cols), BF) for rows, cols in SHARD]
        + [pltpu.VMEM((4, rows, cols), BF) for rows, cols in SHARD]
        + [pltpu.VMEM((2, rows // 2, cols), BF) for rows, cols in SHARD]
        + [pltpu.VMEM((2, rows, cols), BF) for rows, cols in SHARD]
        + [pltpu.SemaphoreType.DMA((2,))]
        + [pltpu.SemaphoreType.DMA((4, 16))] * 2
        + [pltpu.SemaphoreType.DMA((4, 4, 3))] * 2
        + [pltpu.SemaphoreType.DMA((4, 3))] * 2
        + [pltpu.SemaphoreType.DMA((4, 4, 2))] * 2
        + [pltpu.VMEM((1, rows, cols), BF) for rows, cols in SHARD]
        + [pltpu.VMEM((TOK, WID), BF)] * 2
        + [pltpu.VMEM(shape, F32) for shape in SHARD]
        + [pltpu.SemaphoreType.DMA((4,)), pltpu.SemaphoreType.DMA((6,))]
    )
    outs = pl.pallas_call(
        block_kernel,
        name="block",
        out_shape=(
            jax.ShapeDtypeStruct((TOK, WID), BF),
            jax.ShapeDtypeStruct((TOK, WID), BF),
            *(jax.ShapeDtypeStruct(shape, F32) for shape in SHARD),
        ),
        in_specs=[anywhere] * 5 + [smem] * 4 + [anywhere],
        out_specs=(anywhere,) * 6,
        scratch_shapes=scratch,
        compiler_params=pltpu.CompilerParams(
            collective_id=0, has_side_effects=True, vmem_limit_bytes=60 * 2**20
        ),
        cost_estimate=pl.CostEstimate(
            flops=15_000_000_000, bytes_accessed=8_000_000, transcendentals=800_000
        ),
    )(*args[:8], args[8].swapaxes(1, 2), args[9])
    outs = pl.pallas_call(
        write_kernel,
        name="write",
        out_shape=tuple(jax.ShapeDtypeStruct(o.shape, o.dtype) for o in outs),
        in_specs=[anywhere] * 6,
        out_specs=(anywhere,) * 6,
        scratch_shapes=[pltpu.VMEM(o.shape, o.dtype) for o in outs] + [pltpu.SemaphoreType.DMA((2, 12))],
        cost_estimate=pl.CostEstimate(flops=0, bytes_accessed=5_000_000, transcendentals=0),
    )(*outs)
    return (outs[0], outs[1], *(g[None] for g in outs[2:]))


def solution(mesh):
    weight = P("tensor", "dp", None)
    mask = P("tensor", None, None)
    act = P("dp", "tensor")
    return jax.shard_map(
        per_device,
        mesh=mesh,
        in_specs=(act, weight, weight, weight, weight, mask, mask, mask, mask, act),
        out_specs=(act, act, weight, weight, weight, weight),
        check_vma=False,
    )
```
